256 devices in a mesh: rep: 4 (over y_hi, core), fsdp: 64 (over z, x, y_lo).
Axes of the slice: x: 4, y: 4 (y_hi: 2, y_lo: 2; y = y_hi * 2 + y_lo), z: 8, core: 2. Of those that a mesh axis runs over, the one named last changes fastest.
Arguments:
- tokens: bfloat16 [196608, 4096], P(('rep', 'fsdp')), may hold values from -6 to 6
- targets: bfloat16 [196608, 512], P(('rep', 'fsdp')), may hold values from -6 to 6
- params: float32 [16384, 512], P(('rep', 'fsdp')), may hold values from -0.09375 to 0.09375
- moment_one: float32 [16384, 512], P(('rep', 'fsdp')), may hold values from -0.078125 to 0.078125
- moment_two: float32 [16384, 512], P(('rep', 'fsdp')), may hold values from 1e-06 to 0.0001
- anchor: float32 [4096, 512], P('fsdp'), may hold values from -0.09375 to 0.09375
- momentum: float32 [4096, 512], P('fsdp'), may hold values from -0.15625 to 0.15625
- fragment: int32 [512], replicated, may hold values from 0 to 511, each once
- step_offset: int32 [1], replicated, may hold values from 0 to 63
Outputs:
- new_params: float32 [16384, 512], P(('rep', 'fsdp'))
- new_moment_one: float32 [16384, 512], P(('rep', 'fsdp'))
- new_moment_two: float32 [16384, 512], P(('rep', 'fsdp'))
- new_anchor: float32 [4096, 512], P('fsdp')
- new_momentum: float32 [4096, 512], P('fsdp')
The draws below stay inside these ranges and needn't reach their ends.
Inputs may be any that keep to these rules, and one draw needn't show every extreme that they name: fragment names every key column exactly once.
All inputs are finite; a program needn't handle non-finite values.
Results may differ from the reference program's by a relative error of at most 0.0009.
The reference program's roundings to bfloat16 on the way count: a program that leaves them out, or rounds other values in their place, can miss the bound.
Values may be sent and summed in bfloat16 or wider, within the bound.
No kernel may reach another device: no remote copies, remote signals or barrier semaphores. Data moves between devices by JAX's collectives and lax.ppermute only.
A program may use at most 64 MiB of HBM per device.

```python
import math
import jax
import jax.numpy as jnp

DW = 4096
KVW = 512
FRAGW = 128
TOKENS = 49152
N_REP = 4


def steps_of(key, shape, pieces, smallest, top_value):
    factor_of, own = 1.0, jax.random.fold_in(key, 6)
    for position, parts in pieces:
        steps = jnp.exp(jax.random.uniform(jax.random.fold_in(own, position), (parts,), jnp.float32, smallest / len(pieces), top_value / len(pieces)))
        factor_of = factor_of * jnp.repeat(steps, shape[position] // parts).reshape([-1 if axis == position else 1 for axis in range(len(shape))])
    return factor_of


def gaussian(own_key, shape, deviation, limit, cuts=(), dtype=jnp.bfloat16):
    values = jax.random.normal(own_key, shape, jnp.float32) * deviation
    if len(cuts) > 0:
        values = steps_of(own_key, shape, cuts, -0.22, 0.18) * values
    return jnp.clip(values, min=-limit, max=limit).astype(dtype)


def setup_inputs(seed: int = 0) -> dict:
    key_of = jax.random.split(jax.random.key(seed), 10)
    tokens = gaussian(key_of[0], (N_REP * TOKENS, DW), 1.0, 6.0, ((0, 256),))
    targets = gaussian(key_of[1], (N_REP * TOKENS, KVW), 1.0, 6.0, ((0, 256),))
    params = gaussian(key_of[2], (N_REP * DW, KVW), DW ** -0.5, 0.09375, ((0, 256),), jnp.float32)
    moment_one = gaussian(key_of[3], (N_REP * DW, KVW), 0.005, 0.078125, ((0, 256),), jnp.float32)
    moment_two = jnp.clip(jnp.exp(math.log(0.0001) - 4.6051702 * jax.random.uniform(key_of[4], (N_REP * DW, KVW), jnp.float32) ** steps_of(key_of[4], (N_REP * DW, KVW), ((0, 256),), -0.2, 0.2)), 9.999999974752427e-07, 0.0001)
    anchor = gaussian(key_of[5], (DW, KVW), DW ** -0.5, 0.09375, ((0, 64),), jnp.float32)
    momentum = gaussian(key_of[6], (DW, KVW), 0.01, 0.15625, ((0, 64),), jnp.float32)
    fragment = jax.random.permutation(key_of[7], KVW).astype(jnp.int32)
    step_offset = jax.random.randint(key_of[8], (1,), 0, 64).astype(jnp.int32)
    return dict(tokens=tokens, targets=targets, params=params, moment_one=moment_one, moment_two=moment_two, anchor=anchor, momentum=momentum, fragment=fragment, step_offset=step_offset)


def adamw(weights, first, second, grad, tstep):
    first = 0.9 * first + 0.1 * grad
    second = 0.95 * second + 0.05 * grad * grad
    fix_one = 1.0 - jnp.power(jnp.float32(0.9), tstep)
    fix_two = 1.0 - jnp.power(jnp.float32(0.95), tstep)
    update = first / fix_one / (jnp.sqrt(second / fix_two) + 1e-08) + 0.1 * weights
    return (weights - 0.004 * update, first, second)

def reference(tokens, targets, params, moment_one, moment_two, anchor, momentum, fragment, step_offset):
    chosen = fragment[:FRAGW].astype(jnp.int32)
    offset = step_offset[0].astype(jnp.float32)
    base = jnp.take(anchor, chosen, axis=1)
    total = jnp.zeros((DW, FRAGW), jnp.float32)
    for replica in range(N_REP):
        own = jnp.take(params[replica * DW:(replica + 1) * DW], chosen, axis=1)
        total = total + (base - own)
    delta = total / N_REP
    mom_frag = 0.9 * jnp.take(momentum, chosen, axis=1) + delta
    glob = base - 0.7 * (delta + 0.9 * mom_frag)
    new_momentum = momentum.at[:, chosen].set(mom_frag)
    new_anchor = anchor.at[:, chosen].set(glob)
    outs_w, outs_m, outs_v = ([], [], [])
    for replica in range(N_REP):
        weights = params[replica * DW:(replica + 1) * DW]
        first = moment_one[replica * DW:(replica + 1) * DW]
        second = moment_two[replica * DW:(replica + 1) * DW]
        inputs = tokens[replica * TOKENS:(replica + 1) * TOKENS]
        teacher = targets[replica * TOKENS:(replica + 1) * TOKENS].astype(jnp.float32)
        for inner in range(2):
            wb = weights.astype(jnp.bfloat16)
            resid = (jnp.dot(inputs, wb, preferred_element_type=jnp.float32) - teacher).astype(jnp.bfloat16)
            grad = jnp.dot(inputs.T, resid, preferred_element_type=jnp.float32) / TOKENS
            weights, first, second = adamw(weights, first, second, grad, offset + (inner + 1))
            if inner == 0:
                cols = jnp.take(weights, chosen, axis=1)
                weights = weights.at[:, chosen].set(0.5 * (cols + glob))
        outs_w.append(weights)
        outs_m.append(first)
        outs_v.append(second)
    return (jnp.concatenate(outs_w, 0), jnp.concatenate(outs_m, 0), jnp.concatenate(outs_v, 0), new_anchor, new_momentum)
```

```python
import jax
import jax.numpy as jnp
from jax import lax
from jax.experimental import pallas as pl
from jax.experimental.pallas import tpu as pltpu
from jax.sharding import Mesh, PartitionSpec as P

NFRAG = 4
REP = ("yh", "core")
FSDP = ("z", "x", "yl")
NZ, NX = 8, 4
LANES = 128
SHRINK = 2.0 ** -17


def shift(array, axis, by):
    size = lax.axis_size(axis)
    return lax.ppermute(array, axis, [(i, (i + by) % size) for i in range(size)])


def roll_kernel(where, source, by_z, by_x):
    by_z[...] = source[...]
    by_x[...] = source[...]


def rolled(tokens):
    rows = tokens.shape[0]
    where = jnp.stack([lax.axis_index("z"), lax.axis_index("x")]).astype(jnp.int32)
    block = (rows, LANES)
    out = jax.ShapeDtypeStruct(tokens.shape, tokens.dtype)
    return pl.pallas_call(
        roll_kernel,
        grid_spec=pltpu.PrefetchScalarGridSpec(
            num_scalar_prefetch=1,
            grid=(NZ, NX),
            in_specs=[
                pl.BlockSpec(block, lambda i, j, w: (0, lax.rem(w[0] + i, NZ) * NX + lax.rem(w[1] + j, NX)))
            ],
            out_specs=[
                pl.BlockSpec(block, lambda i, j, w: (0, i * NX + j)),
                pl.BlockSpec(block, lambda i, j, w: (0, j * NZ + i)),
            ],
        ),
        out_shape=[out, out],
        cost_estimate=pl.CostEstimate(flops=0, bytes_accessed=3 * tokens.size * 2, transcendentals=0),
    )(where, tokens)


def pair(block, low):
    other = shift(block, "yl", 1)
    return jnp.concatenate([jnp.where(low, block, other), jnp.where(low, other, block)], 0)


def gather_z_last(block, low):
    block = pair(block, low)
    block = jnp.concatenate([block] + [shift(block, "x", -d) for d in range(1, NX)], 0)
    half = block.shape[0] // 2
    ahead, behind = [block], [block]
    for _ in range(NZ // 2 - 1):
        behind.append(shift(behind[-1], "z", 1))
        ahead.append(shift(ahead[-1], "z", -1))
    far = [shift(behind[-1][:half], "z", 1), shift(ahead[-1][half:], "z", -1)]
    return jnp.concatenate(ahead + far + behind[:0:-1], 0)


def gather_x_last(block, low):
    block = pair(block, low)
    block = jnp.concatenate([block] + [shift(block, "z", -d) for d in range(1, NZ)], 0)
    return jnp.concatenate([block] + [shift(block, "x", -d) for d in range(1, NX)], 0)


def coded(array):
    return array.astype(jnp.float16)


def sent(array, axis, by):
    return shift(coded(array), axis, by).astype(jnp.float32)


def halves(total, low):
    total = total.T
    half = total.shape[0] // 2
    mine = jnp.where(low, total[:half], total[half:])
    theirs = jnp.where(low, total[half:], total[:half])
    return mine + shift(theirs, "yl", 1)


def scatter_z_first(terms, low):
    width = terms.shape[1] // NZ
    part = [terms[:, d * width : (d + 1) * width] for d in range(NZ)]
    half = width // 2
    far = NZ // 2
    up = sent(part[far][:, :half], "z", 1)
    down = sent(part[far][:, half:], "z", -1)
    up = jnp.concatenate([part[far - 1][:, :half] + up, part[far - 1][:, half:]], 1)
    down = jnp.concatenate([part[far + 1][:, :half], part[far + 1][:, half:] + down], 1)
    for d in range(far - 2, -1, -1):
        up = sent(up, "z", 1)
        down = sent(down, "z", -1)
        if d:
            up = up + part[d]
            down = down + part[NZ - d]
    total = part[0] + up + down
    width = width // NX
    part = [total[:, d * width : (d + 1) * width] for d in range(NX)]
    total = part[0]
    for d in range(1, NX):
        total = total + shift(part[d], "x", d)
    return halves(total, low)


def scatter_x_first(terms, low):
    width = terms.shape[1] // NX
    total = terms[:, :width]
    for d in range(1, NX):
        total = total + sent(terms[:, d * width : (d + 1) * width], "x", d)
    width = width // NZ
    parts = total
    total = parts[:, :width]
    for d in range(1, NZ):
        total = total + sent(parts[:, d * width : (d + 1) * width], "z", d)
    return halves(total, low)


def adamw(weights, first, second, grad, tstep):
    first = 0.9 * first + 0.1 * grad
    second = 0.95 * second + 0.05 * grad * grad
    fix_one = 1.0 - jnp.power(jnp.float32(0.9), tstep)
    fix_two = 1.0 - jnp.power(jnp.float32(0.95), tstep)
    update = first / fix_one / (jnp.sqrt(second / fix_two) + 1e-08) + 0.1 * weights
    return (weights - 0.004 * update, first, second)


def partial_gradient(tokens, weights, targets):
    outputs = jnp.dot(tokens, weights, preferred_element_type=jnp.float32)
    resid = (outputs - targets.astype(jnp.float32)).astype(jnp.bfloat16)
    terms = lax.dot_general(resid, tokens, (((0,), (0,)), ((), ())), preferred_element_type=jnp.float32)
    return terms * SHRINK


def body(tokens, targets, params, moment_one, moment_two, anchor, momentum, fragment, step_offset):
    width = params.shape[1]
    half = width // 2
    chosen = fragment[: width // NFRAG]
    offset = step_offset[0].astype(jnp.float32)
    replicas = lax.axis_size("yh") * lax.axis_size("core")
    devices = NZ * NX * lax.axis_size("yl")
    total_tokens = tokens.shape[0] * devices
    low = lax.axis_index("yl") == 0

    by_z, by_x = rolled(tokens)
    columns = [slice(0, half), slice(half, width)]
    ways = [(by_z, gather_z_last, scatter_z_first), (by_x, gather_x_last, scatter_x_first)]

    mask = jnp.any(jnp.arange(width, dtype=jnp.int32)[:, None] == chosen[None, :], axis=1)[None, :]
    delta = anchor - params
    delta = delta + shift(delta, "core", 1)
    delta = (delta + shift(delta, "yh", 1)) / replicas
    new_momentum = jnp.where(mask, 0.9 * momentum + delta, momentum)
    new_anchor = jnp.where(mask, anchor - 0.7 * (delta + 0.9 * new_momentum), anchor)

    outs = []
    for cols, (inputs, gather, scatter) in zip(columns, ways):
        weights, first, second = params[:, cols], moment_one[:, cols], moment_two[:, cols]
        for inner in range(2):
            whole = gather(weights.astype(jnp.bfloat16), low)
            terms = partial_gradient(inputs, whole, targets[:, cols])
            grad = scatter(terms, low) / (SHRINK * total_tokens)
            weights, first, second = adamw(weights, first, second, grad, offset + (inner + 1))
            if inner == 0:
                weights = jnp.where(mask[:, cols], 0.5 * (weights + new_anchor[:, cols]), weights)
        outs.append((weights, first, second))
    weights, first, second = (jnp.concatenate(o, 1) for o in zip(*outs))
    return (weights, first, second, new_anchor, new_momentum)


def solution(mesh):
    mesh = Mesh(mesh.devices.reshape(2, 2, NZ, NX, 2), REP + FSDP)
    both, own = P(REP + FSDP, None), P(FSDP, None)
    return jax.shard_map(
        body,
        mesh=mesh,
        in_specs=(both, both, both, both, both, own, own, P(), P()),
        out_specs=(both, both, both, own, own),
        check_vma=False,
    )
```

```python
import functools

import jax
import jax.numpy as jnp
from jax import lax
from jax.experimental import pallas as pl
from jax.experimental.pallas import tpu as pltpu
from jax.sharding import Mesh, PartitionSpec as P

NFRAG = 4
REP = ("yh", "core")
FSDP = ("z", "x", "yl")
NZ, NX, NY = 8, 4, 2
SIZE = {"z": NZ, "x": NX, "yl": NY}
SHRINK = 2.0 ** -17
SENT = jnp.float16
GROUPS = (("z", 0, 256), ("x", 256, 512))
UNIT = 128


def shift(array, axis, by):
    size = lax.axis_size(axis)
    return lax.ppermute(array, axis, [(i, (i + by) % size) for i in range(size)])


def after(array, *others):
    return lax.optimization_barrier((array,) + others)[0]


def gradient_kernel(come, leave, first, where_ref, tokens_ref, targets_ref, *refs):
    blocks, (out_ref, whole_ref, acc_ref, resid_ref) = refs[:-4], refs[-4:]
    step, x = pl.program_id(0), where_ref[0]
    tiles = pl.num_programs(0) // 2
    depth = tokens_ref.shape[1]
    pieces = [(d, k) for d in range(NX) for k in range(depth // (NX * UNIT))]

    @pl.when(step < tiles)
    def _():
        for d, k in pieces:
            place = k * NX * UNIT + lax.rem(x + d, NX) * UNIT
            ref, row = (blocks[d], k * UNIT) if come == "x" else (blocks[0], (k * NX + d) * UNIT)
            whole_ref[pl.ds(pl.multiple_of(place, UNIT), UNIT), :] = ref[row : row + UNIT, :]
        term = jnp.dot(tokens_ref[...], whole_ref[...], preferred_element_type=jnp.float32)

        @pl.when(step == 0)
        def _():
            acc_ref[...] = term

        @pl.when(step > 0)
        def _():
            acc_ref[...] += term

    @pl.when(step == tiles)
    def _():
        targets = targets_ref[:, first : first + acc_ref.shape[1]].astype(jnp.float32)
        resid_ref[...] = (acc_ref[...] - targets).astype(jnp.bfloat16).T

    @pl.when(step >= tiles)
    def _():
        for k in range(depth // (NX * UNIT)):
            columns = tokens_ref[:, k * NX * UNIT : (k + 1) * NX * UNIT]
            term = jnp.dot(resid_ref[...], columns, preferred_element_type=jnp.float32)
            term = (term * SHRINK).T
            for j in range(NX):
                piece = term[j * UNIT : (j + 1) * UNIT]
                slot = lax.rem(j + NX - x, NX)
                if leave == "x":
                    out_ref[slot, k * UNIT : (k + 1) * UNIT, :] = piece
                else:
                    out_ref[pl.ds(pl.multiple_of((k * NX + slot) * UNIT, UNIT), UNIT), :] = piece


def partial_gradient(come, leave, first, tokens, targets, blocks, where):
    rows, width = tokens.shape
    cols = blocks[0].shape[1]
    tiles = 4
    depth = width // tiles
    if come == "x":
        weights = [pl.BlockSpec((depth // NX, cols), lambda i, w: (jnp.minimum(i, tiles - 1), 0))] * NX
    else:
        weights = [pl.BlockSpec((depth, cols), lambda i, w: (jnp.minimum(i, tiles - 1), 0))]
    if leave == "x":
        out_block = pl.BlockSpec((NX, depth // NX, cols), lambda i, w: (0, jnp.maximum(i - tiles, 0), 0))
        out_shape = (NX, width // NX, cols)
    else:
        out_block = pl.BlockSpec((depth, cols), lambda i, w: (jnp.maximum(i - tiles, 0), 0))
        out_shape = (width, cols)
    return pl.pallas_call(
        functools.partial(gradient_kernel, come, leave, first),
        grid_spec=pltpu.PrefetchScalarGridSpec(
            num_scalar_prefetch=1,
            grid=(2 * tiles,),
            in_specs=[
                pl.BlockSpec((rows, depth), lambda i, w: (0, lax.rem(i, tiles))),
                pl.BlockSpec(targets.shape, lambda i, w: (0, 0)),
            ]
            + weights,
            out_specs=out_block,
            scratch_shapes=[
                pltpu.VMEM((depth, cols), jnp.bfloat16),
                pltpu.VMEM((rows, cols), jnp.float32),
                pltpu.VMEM((cols, rows), jnp.bfloat16),
            ],
        ),
        out_shape=jax.ShapeDtypeStruct(out_shape, jnp.float32),
        compiler_params=pltpu.CompilerParams(vmem_limit_bytes=20 * 2**20),
        cost_estimate=pl.CostEstimate(flops=4 * rows * width * cols, bytes_accessed=4 * rows * width, transcendentals=0),
    )(where, tokens, targets, *blocks)


def sent(array, axis, by):
    return shift(array.astype(SENT), axis, by).astype(jnp.float32)


def gather_by_z(block, low):
    other = shift(block, "yl", 1)
    block = jnp.concatenate([jnp.where(low, block, other), jnp.where(low, other, block)], 0)
    block = jnp.concatenate([block] + [shift(block, "x", -d) for d in range(1, NX)], 0)
    return [lax.all_gather(block, "z", axis=0, tiled=True)]


def gather_by_x(block):
    copies = jnp.broadcast_to(block[None], (NZ * NY,) + block.shape)
    block = lax.all_to_all(copies, ("z", "yl"), 0, 0).reshape(-1, block.shape[1])
    return [block] + [shift(block, "x", -d) for d in range(1, NX)]


def scatter_by_x(part):
    total = part[0]
    for d in range(1, NX):
        total = total + sent(part[d], "x", d)
    return total


def scatter_near_x(total):
    terms = total.astype(SENT).reshape(NZ * NY, -1, total.shape[1])
    return jnp.sum(lax.all_to_all(terms, ("z", "yl"), 0, 0).astype(jnp.float32), 0)


def scatter_by_z(terms):
    width = terms.shape[0] // NZ
    mine = lax.axis_index("z")

    def part(d, low=0, high=width):
        return lax.dynamic_slice_in_dim(terms, lax.rem(mine + d, NZ) * width + low, high - low, 0)

    half = width // 2
    mid = NZ // 2
    up = sent(part(mid, 0, half), "z", 1)
    down = sent(part(mid, half, width), "z", -1)
    up = jnp.concatenate([part(mid - 1, 0, half) + up, part(mid - 1, half, width)], 0)
    down = jnp.concatenate([part(mid + 1, 0, half), part(mid + 1, half, width) + down], 0)
    for d in range(mid - 2, -1, -1):
        up = sent(up, "z", 1)
        down = sent(down, "z", -1)
        if d:
            up = up + part(d)
            down = down + part(NZ - d)
    return part(0) + up + down


def scatter_near_z(total, low):
    sums = total[:UNIT]
    for d in range(1, NX):
        sums = sums + shift(total[d * UNIT : (d + 1) * UNIT], "x", d)
    half = UNIT // 2
    mine = jnp.where(low, sums[:half], sums[half:])
    theirs = jnp.where(low, sums[half:], sums[:half])
    return mine + shift(theirs, "yl", 1)


def adamw(weights, first, second, grad, tstep):
    first = 0.9 * first + 0.1 * grad
    second = 0.95 * second + 0.05 * grad * grad
    fix_one = 1.0 - jnp.power(jnp.float32(0.9), tstep)
    fix_two = 1.0 - jnp.power(jnp.float32(0.95), tstep)
    update = first / fix_one / (jnp.sqrt(second / fix_two) + 1e-08) + 0.1 * weights
    return (weights - 0.004 * update, first, second)


def body(tokens, targets, params, moment_one, moment_two, anchor, momentum, fragment, step_offset):
    width = params.shape[1]
    chosen = fragment[: width // NFRAG]
    offset = step_offset[0].astype(jnp.float32)
    replicas = lax.axis_size(REP)
    total_tokens = tokens.shape[0] * lax.axis_size(FSDP)
    where = jnp.reshape(lax.axis_index("x"), (1,)).astype(jnp.int32)

    mask = jnp.any(jnp.arange(width, dtype=jnp.int32)[:, None] == chosen[None, :], axis=1)[None, :]
    delta = anchor - params
    delta = delta + shift(delta, "core", 1)
    delta = (delta + shift(delta, "yh", 1)) / replicas
    new_momentum = jnp.where(mask, 0.9 * momentum + delta, momentum)
    new_anchor = jnp.where(mask, anchor - 0.7 * (delta + 0.9 * new_momentum), anchor)

    low = lax.axis_index("yl") == 0
    state = [[a[:, start:stop] for a in (params, moment_one, moment_two)] for far, start, stop in GROUPS]
    for inner in range(2):
        small = [state[number][0].astype(jnp.bfloat16) for number in range(2)]
        by_x = gather_by_x(small[1])
        by_z = gather_by_z(small[0], low)
        z_terms = partial_gradient("z", "z", GROUPS[0][1], tokens, targets, by_z, where)
        by_x[0] = after(by_x[0], z_terms)
        x_terms = partial_gradient("x", "x", GROUPS[1][1], tokens, targets, by_x, where)
        z_sum = scatter_near_z(scatter_by_z(z_terms), low)
        x_sum = scatter_near_x(scatter_by_x(x_terms))
        for number, summed in ((1, x_sum), (0, z_sum)):
            far, start, stop = GROUPS[number]
            cols = slice(start, stop)
            weights, first, second = state[number]
            grad = summed / (SHRINK * total_tokens)
            weights, first, second = adamw(weights, first, second, grad, offset + (inner + 1))
            if inner == 0:
                weights = jnp.where(mask[:, cols], 0.5 * (weights + new_anchor[:, cols]), weights)
            state[number] = weights, first, second
    weights, first, second = (jnp.concatenate(o, 1) for o in zip(*state))
    return (weights, first, second, new_anchor, new_momentum)


def solution(mesh):
    mesh = Mesh(mesh.devices.reshape(2, 2, NZ, NX, NY), REP + FSDP)
    both, own = P(REP + FSDP, None), P(FSDP, None)
    return jax.shard_map(
        body,
        mesh=mesh,
        in_specs=(both, both, both, both, both, own, own, P(), P()),
        out_specs=(both, both, both, own, own),
        check_vma=False,
    )
```

```python
import functools

import jax
import jax.numpy as jnp
from jax import lax
from jax.experimental import pallas as pl
from jax.experimental.pallas import tpu as pltpu
from jax.sharding import Mesh, PartitionSpec as P

NFRAG = 4
REP = ("yh", "core")
FSDP = ("z", "x", "yl")
NZ, NX, NY = 8, 4, 2
SIZE = {"z": NZ, "x": NX, "yl": NY}
SHRINK = 2.0 ** -17
SENT = jnp.float16
GROUPS = (("z", 0, 256), ("x", 256, 512))
UNIT = 128


def shift(array, axis, by):
    size = lax.axis_size(axis)
    return lax.ppermute(array, axis, [(i, (i + by) % size) for i in range(size)])


def after(array, *others):
    return lax.optimization_barrier((array,) + others)[0]


def gradient_kernel(come, leave, first, where_ref, tokens_ref, targets_ref, *refs):
    blocks, (out_ref, whole_ref, acc_ref, resid_ref) = refs[:-4], refs[-4:]
    step, x = pl.program_id(0), where_ref[0]
    tiles = pl.num_programs(0) // 2
    depth = tokens_ref.shape[1]
    pieces = [(d, k) for d in range(NX) for k in range(depth // (NX * UNIT))]

    @pl.when(step < tiles)
    def _():
        for d, k in pieces:
            place = k * NX * UNIT + lax.rem(x + d, NX) * UNIT
            ref, row = (blocks[d], k * UNIT) if come == "x" else (blocks[0], (k * NX + d) * UNIT)
            whole_ref[pl.ds(pl.multiple_of(place, UNIT), UNIT), :] = ref[row : row + UNIT, :]
        term = jnp.dot(tokens_ref[...], whole_ref[...], preferred_element_type=jnp.float32)

        @pl.when(step == 0)
        def _():
            acc_ref[...] = term

        @pl.when(step > 0)
        def _():
            acc_ref[...] += term

    @pl.when(step == tiles)
    def _():
        targets = targets_ref[:, first : first + acc_ref.shape[1]].astype(jnp.float32)
        resid_ref[...] = (acc_ref[...] - targets).astype(jnp.bfloat16).T

    @pl.when(step >= tiles)
    def _():
        for k in range(depth // (NX * UNIT)):
            columns = tokens_ref[:, k * NX * UNIT : (k + 1) * NX * UNIT]
            term = jnp.dot(resid_ref[...], columns, preferred_element_type=jnp.float32)
            term = (term * SHRINK).T
            for j in range(NX):
                piece = term[j * UNIT : (j + 1) * UNIT]
                slot = lax.rem(j + NX - x, NX)
                if leave == "x":
                    out_ref[slot, k * UNIT : (k + 1) * UNIT, :] = piece
                else:
                    out_ref[pl.ds(pl.multiple_of((k * NX + slot) * UNIT, UNIT), UNIT), :] = piece


def partial_gradient(come, leave, first, tokens, targets, blocks, where):
    rows, width = tokens.shape
    cols = blocks[0].shape[1]
    tiles = 4
    depth = width // tiles
    if come == "x":
        weights = [pl.BlockSpec((depth // NX, cols), lambda i, w: (jnp.minimum(i, tiles - 1), 0))] * NX
    else:
        weights = [pl.BlockSpec((depth, cols), lambda i, w: (jnp.minimum(i, tiles - 1), 0))]
    if leave == "x":
        out_block = pl.BlockSpec((NX, depth // NX, cols), lambda i, w: (0, jnp.maximum(i - tiles, 0), 0))
        out_shape = (NX, width // NX, cols)
    else:
        out_block = pl.BlockSpec((depth, cols), lambda i, w: (jnp.maximum(i - tiles, 0), 0))
        out_shape = (width, cols)
    return pl.pallas_call(
        functools.partial(gradient_kernel, come, leave, first),
        grid_spec=pltpu.PrefetchScalarGridSpec(
            num_scalar_prefetch=1,
            grid=(2 * tiles,),
            in_specs=[
                pl.BlockSpec((rows, depth), lambda i, w: (0, lax.rem(i, tiles))),
                pl.BlockSpec(targets.shape, lambda i, w: (0, 0)),
            ]
            + weights,
            out_specs=out_block,
            scratch_shapes=[
                pltpu.VMEM((depth, cols), jnp.bfloat16),
                pltpu.VMEM((rows, cols), jnp.float32),
                pltpu.VMEM((cols, rows), jnp.bfloat16),
            ],
        ),
        out_shape=jax.ShapeDtypeStruct(out_shape, jnp.float32),
        compiler_params=pltpu.CompilerParams(vmem_limit_bytes=20 * 2**20),
        cost_estimate=pl.CostEstimate(flops=4 * rows * width * cols, bytes_accessed=4 * rows * width, transcendentals=0),
    )(where, tokens, targets, *blocks)


def sent(array, axis, by):
    return shift(array.astype(SENT), axis, by).astype(jnp.float32)


def gather_by_z(block, low):
    other = shift(block, "yl", 1)
    block = jnp.concatenate([jnp.where(low, block, other), jnp.where(low, other, block)], 0)
    block = jnp.concatenate([block] + [shift(block, "x", -d) for d in range(1, NX)], 0)
    return [lax.all_gather(block, "z", axis=0, tiled=True)]


def gather_by_x(block):
    copies = jnp.broadcast_to(block[None], (NZ * NY,) + block.shape)
    block = lax.all_to_all(copies, ("z", "yl"), 0, 0).reshape(-1, block.shape[1])
    return [block] + [shift(block, "x", -d) for d in range(1, NX)]


def scatter_by_x(part):
    total = part[0]
    for d in range(1, NX):
        total = total + sent(part[d], "x", d)
    return total


def scatter_near_x(total):
    terms = total.astype(SENT).reshape(NZ * NY, -1, total.shape[1])
    return jnp.sum(lax.all_to_all(terms, ("z", "yl"), 0, 0).astype(jnp.float32), 0)


def scatter_by_z(terms):
    width = terms.shape[0] // NZ
    mine = lax.axis_index("z")

    def part(d, low=0, high=width):
        return lax.dynamic_slice_in_dim(terms, lax.rem(mine + d, NZ) * width + low, high - low, 0)

    half = width // 2
    mid = NZ // 2
    up = sent(part(mid, 0, half), "z", 1)
    down = sent(part(mid, half, width), "z", -1)
    up = jnp.concatenate([part(mid - 1, 0, half) + up, part(mid - 1, half, width)], 0)
    down = jnp.concatenate([part(mid + 1, 0, half), part(mid + 1, half, width) + down], 0)
    for d in range(mid - 2, -1, -1):
        up = sent(up, "z", 1)
        down = sent(down, "z", -1)
        if d:
            up = up + part(d)
            down = down + part(NZ - d)
    return part(0) + up + down


def scatter_near_z(total, low):
    sums = total[:UNIT]
    for d in range(1, NX):
        sums = sums + shift(total[d * UNIT : (d + 1) * UNIT], "x", d)
    half = UNIT // 2
    mine = jnp.where(low, sums[:half], sums[half:])
    theirs = jnp.where(low, sums[half:], sums[:half])
    return mine + shift(theirs, "yl", 1)


def adamw(weights, first, second, grad, tstep):
    first = 0.9 * first + 0.1 * grad
    second = 0.95 * second + 0.05 * grad * grad
    fix_one = 1.0 - jnp.power(jnp.float32(0.9), tstep)
    fix_two = 1.0 - jnp.power(jnp.float32(0.95), tstep)
    update = first / fix_one / (jnp.sqrt(second / fix_two) + 1e-08) + 0.1 * weights
    return (weights - 0.004 * update, first, second)


def body(tokens, targets, params, moment_one, moment_two, anchor, momentum, fragment, step_offset):
    width = params.shape[1]
    chosen = fragment[: width // NFRAG]
    offset = step_offset[0].astype(jnp.float32)
    replicas = lax.axis_size(REP)
    total_tokens = tokens.shape[0] * lax.axis_size(FSDP)
    where = jnp.reshape(lax.axis_index("x"), (1,)).astype(jnp.int32)

    mask = jnp.any(jnp.arange(width, dtype=jnp.int32)[:, None] == chosen[None, :], axis=1)[None, :]
    delta = anchor - params
    delta = delta + shift(delta, "core", 1)
    delta = (delta + shift(delta, "yh", 1)) / replicas
    new_momentum = jnp.where(mask, 0.9 * momentum + delta, momentum)
    new_anchor = jnp.where(mask, anchor - 0.7 * (delta + 0.9 * new_momentum), anchor)

    low = lax.axis_index("yl") == 0
    state = [[a[:, start:stop] for a in (params, moment_one, moment_two)] for far, start, stop in GROUPS]
    for inner in range(2):
        small = [state[number][0].astype(jnp.bfloat16) for number in range(2)]
        by_x = gather_by_x(small[1])
        by_z = gather_by_z(small[0], low)
        if inner == 0:
            by_z[0] = after(by_z[0], new_anchor)
        z_terms = partial_gradient("z", "z", GROUPS[0][1], tokens, targets, by_z, where)
        by_x[0] = after(by_x[0], z_terms)
        x_terms = partial_gradient("x", "x", GROUPS[1][1], tokens, targets, by_x, where)
        z_sum = scatter_near_z(scatter_by_z(z_terms), low)
        x_sum = scatter_near_x(scatter_by_x(x_terms))
        for number, summed in ((1, x_sum), (0, z_sum)):
            far, start, stop = GROUPS[number]
            cols = slice(start, stop)
            weights, first, second = state[number]
            grad = summed / (SHRINK * total_tokens)
            weights, first, second = adamw(weights, first, second, grad, offset + (inner + 1))
            if inner == 0:
                weights = jnp.where(mask[:, cols], 0.5 * (weights + new_anchor[:, cols]), weights)
            state[number] = weights, first, second
    weights, first, second = (jnp.concatenate(o, 1) for o in zip(*state))
    return (weights, first, second, new_anchor, new_momentum)


def solution(mesh):
    mesh = Mesh(mesh.devices.reshape(2, 2, NZ, NX, NY), REP + FSDP)
    both, own = P(REP + FSDP, None), P(FSDP, None)
    return jax.shard_map(
        body,
        mesh=mesh,
        in_specs=(both, both, both, both, both, own, own, P(), P()),
        out_specs=(both, both, both, own, own),
        check_vma=False,
    )
```

```python
import functools

import jax
import jax.numpy as jnp
from jax import lax
from jax.experimental import pallas as pl
from jax.experimental.pallas import tpu as pltpu
from jax.sharding import Mesh, PartitionSpec as P

NFRAG = 4
REP = ("yh", "core")
FSDP = ("z", "x", "yl")
NZ, NX, NY = 8, 4, 2
SIZE = {"z": NZ, "x": NX, "yl": NY}
SHRINK = 2.0 ** -17
SENT = jnp.float16
GROUPS = (("z", 0, 256), ("x", 256, 512))
UNIT = 128


def shift(array, axis, by):
    size = lax.axis_size(axis)
    return lax.ppermute(array, axis, [(i, (i + by) % size) for i in range(size)])


def after(array, *others):
    return lax.optimization_barrier((array,) + others)[0]


def gradient_kernel(come, leave, first, where_ref, tokens_ref, targets_ref, *refs):
    blocks, (out_ref, whole_ref, acc_ref, resid_ref) = refs[:-4], refs[-4:]
    step, x = pl.program_id(0), where_ref[0]
    tiles = pl.num_programs(0) // 2
    depth = tokens_ref.shape[1]
    pieces = [(d, k) for d in range(NX) for k in range(depth // (NX * UNIT))]

    @pl.when(step < tiles)
    def _():
        for d, k in pieces:
            place = k * NX * UNIT + lax.rem(x + d, NX) * UNIT
            ref, row = (blocks[d], k * UNIT) if come == "x" else (blocks[0], (k * NX + d) * UNIT)
            whole_ref[pl.ds(pl.multiple_of(place, UNIT), UNIT), :] = ref[row : row + UNIT, :]
        term = jnp.dot(tokens_ref[...], whole_ref[...], preferred_element_type=jnp.float32)

        @pl.when(step == 0)
        def _():
            acc_ref[...] = term

        @pl.when(step > 0)
        def _():
            acc_ref[...] += term

    @pl.when(step == tiles)
    def _():
        targets = targets_ref[:, first : first + acc_ref.shape[1]].astype(jnp.float32)
        resid_ref[...] = (acc_ref[...] - targets).astype(jnp.bfloat16).T

    @pl.when(step >= tiles)
    def _():
        for k in range(depth // (NX * UNIT)):
            columns = tokens_ref[:, k * NX * UNIT : (k + 1) * NX * UNIT]
            term = jnp.dot(resid_ref[...], columns, preferred_element_type=jnp.float32)
            term = (term * SHRINK).T
            for j in range(NX):
                piece = term[j * UNIT : (j + 1) * UNIT]
                slot = lax.rem(j + NX - x, NX)
                if leave == "x":
                    out_ref[slot, k * UNIT : (k + 1) * UNIT, :] = piece
                else:
                    out_ref[pl.ds(pl.multiple_of((k * NX + slot) * UNIT, UNIT), UNIT), :] = piece


def partial_gradient(come, leave, first, tokens, targets, blocks, where):
    rows, width = tokens.shape
    cols = blocks[0].shape[1]
    tiles = 2
    depth = width // tiles
    if come == "x":
        weights = [pl.BlockSpec((depth // NX, cols), lambda i, w: (jnp.minimum(i, tiles - 1), 0))] * NX
    else:
        weights = [pl.BlockSpec((depth, cols), lambda i, w: (jnp.minimum(i, tiles - 1), 0))]
    if leave == "x":
        out_block = pl.BlockSpec((NX, depth // NX, cols), lambda i, w: (0, jnp.maximum(i - tiles, 0), 0))
        out_shape = (NX, width // NX, cols)
    else:
        out_block = pl.BlockSpec((depth, cols), lambda i, w: (jnp.maximum(i - tiles, 0), 0))
        out_shape = (width, cols)
    return pl.pallas_call(
        functools.partial(gradient_kernel, come, leave, first),
        grid_spec=pltpu.PrefetchScalarGridSpec(
            num_scalar_prefetch=1,
            grid=(2 * tiles,),
            in_specs=[
                pl.BlockSpec((rows, depth), lambda i, w: (0, lax.rem(i, tiles))),
                pl.BlockSpec(targets.shape, lambda i, w: (0, 0)),
            ]
            + weights,
            out_specs=out_block,
            scratch_shapes=[
                pltpu.VMEM((depth, cols), jnp.bfloat16),
                pltpu.VMEM((rows, cols), jnp.float32),
                pltpu.VMEM((cols, rows), jnp.bfloat16),
            ],
        ),
        out_shape=jax.ShapeDtypeStruct(out_shape, jnp.float32),
        compiler_params=pltpu.CompilerParams(vmem_limit_bytes=20 * 2**20),
        cost_estimate=pl.CostEstimate(flops=4 * rows * width * cols, bytes_accessed=4 * rows * width, transcendentals=0),
    )(where, tokens, targets, *blocks)


def sent(array, axis, by):
    return shift(array.astype(SENT), axis, by).astype(jnp.float32)


def gather_by_z(block, low):
    other = shift(block, "yl", 1)
    block = jnp.concatenate([jnp.where(low, block, other), jnp.where(low, other, block)], 0)
    block = jnp.concatenate([block] + [shift(block, "x", -d) for d in range(1, NX)], 0)
    return [lax.all_gather(block, "z", axis=0, tiled=True)]


def gather_by_x(block):
    copies = jnp.broadcast_to(block[None], (NZ * NY,) + block.shape)
    block = lax.all_to_all(copies, ("z", "yl"), 0, 0).reshape(-1, block.shape[1])
    return [block] + [shift(block, "x", -d) for d in range(1, NX)]


def scatter_by_x(part):
    total = part[0]
    for d in range(1, NX):
        total = total + sent(part[d], "x", d)
    return total


def scatter_near_x(total):
    terms = total.astype(SENT).reshape(NZ * NY, -1, total.shape[1])
    return jnp.sum(lax.all_to_all(terms, ("z", "yl"), 0, 0).astype(jnp.float32), 0)


def scatter_by_z(terms):
    width = terms.shape[0] // NZ
    mine = lax.axis_index("z")

    def part(d, low=0, high=width):
        return lax.dynamic_slice_in_dim(terms, lax.rem(mine + d, NZ) * width + low, high - low, 0)

    half = width // 2
    mid = NZ // 2
    up = sent(part(mid, 0, half), "z", 1)
    down = sent(part(mid, half, width), "z", -1)
    up = jnp.concatenate([part(mid - 1, 0, half) + up, part(mid - 1, half, width)], 0)
    down = jnp.concatenate([part(mid + 1, 0, half), part(mid + 1, half, width) + down], 0)
    for d in range(mid - 2, -1, -1):
        up = sent(up, "z", 1)
        down = sent(down, "z", -1)
        if d:
            up = up + part(d)
            down = down + part(NZ - d)
    return part(0) + up + down


def scatter_near_z(total, low):
    sums = total[:UNIT]
    for d in range(1, NX):
        sums = sums + sent(total[d * UNIT : (d + 1) * UNIT], "x", d)
    half = UNIT // 2
    mine = jnp.where(low, sums[:half], sums[half:])
    theirs = jnp.where(low, sums[half:], sums[:half])
    return mine + sent(theirs, "yl", 1)


def adamw(weights, first, second, grad, tstep):
    first = 0.9 * first + 0.1 * grad
    second = 0.95 * second + 0.05 * grad * grad
    fix_one = 1.0 - jnp.power(jnp.float32(0.9), tstep)
    fix_two = 1.0 - jnp.power(jnp.float32(0.95), tstep)
    update = first / fix_one / (jnp.sqrt(second / fix_two) + 1e-08) + 0.1 * weights
    return (weights - 0.004 * update, first, second)


def body(tokens, targets, params, moment_one, moment_two, anchor, momentum, fragment, step_offset):
    width = params.shape[1]
    chosen = fragment[: width // NFRAG]
    offset = step_offset[0].astype(jnp.float32)
    replicas = lax.axis_size(REP)
    total_tokens = tokens.shape[0] * lax.axis_size(FSDP)
    where = jnp.reshape(lax.axis_index("x"), (1,)).astype(jnp.int32)

    mask = jnp.any(jnp.arange(width, dtype=jnp.int32)[:, None] == chosen[None, :], axis=1)[None, :]
    delta = anchor - params
    delta = delta + shift(delta, "core", 1)
    delta = (delta + shift(delta, "yh", 1)) / replicas
    new_momentum = jnp.where(mask, 0.9 * momentum + delta, momentum)
    new_anchor = jnp.where(mask, anchor - 0.7 * (delta + 0.9 * new_momentum), anchor)

    low = lax.axis_index("yl") == 0
    state = [[a[:, start:stop] for a in (params, moment_one, moment_two)] for far, start, stop in GROUPS]
    for inner in range(2):
        small = [state[number][0].astype(jnp.bfloat16) for number in range(2)]
        by_x = gather_by_x(small[1])
        by_z = gather_by_z(small[0], low)
        if inner == 0:
            by_z[0] = after(by_z[0], new_anchor)
        z_terms = partial_gradient("z", "z", GROUPS[0][1], tokens, targets, by_z, where)
        by_x[0] = after(by_x[0], z_terms)
        x_terms = partial_gradient("x", "x", GROUPS[1][1], tokens, targets, by_x, where)
        z_sum = scatter_near_z(scatter_by_z(z_terms), low)
        x_sum = scatter_near_x(scatter_by_x(x_terms))
        for number, summed in ((1, x_sum), (0, z_sum)):
            far, start, stop = GROUPS[number]
            cols = slice(start, stop)
            weights, first, second = state[number]
            grad = summed / (SHRINK * total_tokens)
            weights, first, second = adamw(weights, first, second, grad, offset + (inner + 1))
            if inner == 0:
                weights = jnp.where(mask[:, cols], 0.5 * (weights + new_anchor[:, cols]), weights)
            state[number] = weights, first, second
    weights, first, second = (jnp.concatenate(o, 1) for o in zip(*state))
    return (weights, first, second, new_anchor, new_momentum)


def solution(mesh):
    mesh = Mesh(mesh.devices.reshape(2, 2, NZ, NX, NY), REP + FSDP)
    both, own = P(REP + FSDP, None), P(FSDP, None)
    return jax.shard_map(
        body,
        mesh=mesh,
        in_specs=(both, both, both, both, both, own, own, P(), P()),
        out_specs=(both, both, both, own, own),
        check_vma=False,
    )
```
